32 devices in a mesh: tm: 8 (over y, x, core), space: 4 (over z).
Axes of the slice: x: 2, y: 2, z: 4, core: 2. Of those that a mesh axis runs over, the one named last changes fastest.
Arguments:
- queries: bfloat16 [8, 1024, 512], P('tm', 'space'), may hold values from -8 to 8
- key_tokens: bfloat16 [8, 1024, 512], P('tm', 'space'), may hold values from -8 to 8
- values: bfloat16 [8, 1024, 512], P('tm', 'space'), may hold values from -8 to 8
- near_list: int32 [8, 4, 8], replicated, may hold values from 0 to 11, as said below
- near_count: int32 [8, 4], replicated, may hold values from 1 to 8, as said below
- dist_band: int32 [8], replicated, may hold values from 0 to 3, as said below
- band_factor: int32 [3], replicated, may hold values from 1 to 4, as said below
Outputs:
- attended: bfloat16 [8, 1024, 512], P('tm', 'space')
The draws below stay inside these ranges and needn't reach their ends.
Inputs may be any that keep to these rules, and one draw needn't show every extreme that they name: `near_list`: each entry is distinct within its list, never names a frame outside 0 to 7, and the first entry of block b is block b of the same frame. `near_count`: some query block of some frame lists 8 live blocks. `dist_band`: nondecreasing in the distance; 0 exactly for distances 0 and 1, 3 at distance 8 - 1. `band_factor`: each entry is 1, 2 or 4, and some entry is 4.
All inputs are finite; a program needn't handle non-finite values.
Results may differ from the reference program's by a relative error of at most 0.0028.
The reference program's roundings to bfloat16 on the way count: a program that leaves them out, or rounds other values in their place, can miss the bound.
Values may be sent and summed in bfloat16 or wider, within the bound.
A program may use at most 64 MiB of HBM per device.

```python
import math
import jax
import jax.numpy as jnp
from jax import lax

HD = 128
POOL = 128
LIST = 8
NBANDS = 3
HEADS = 4
FRAMES = 8
FTOK = 1024
BLOCKS = 4


def group_common(key):
    group_count = FTOK // POOL
    common = jax.random.normal(key, (FRAMES, group_count, 1, HEADS * HD))
    common = jnp.clip(common, -4.0, 4.0)
    return jnp.broadcast_to(common, (FRAMES, group_count, POOL, HEADS * HD)).reshape(FRAMES, FTOK, HEADS * HD)


def drawn_pair(key):
    shape_all = (FRAMES, FTOK, HEADS * HD)
    query_key = jax.random.fold_in(key, 11)
    token_key = jax.random.fold_in(key, 12)
    shared_key = jax.random.fold_in(key, 14)
    key_common = group_common(shared_key)
    query_draw = jnp.clip(jax.random.normal(query_key, shape_all), -6.0, 6.0)
    key_noise = jnp.clip(jax.random.normal(token_key, shape_all), -6.0, 6.0)
    key_draw = 0.85 * key_common + 0.5 * key_noise
    return (query_draw, key_draw)


def draw_queries(key, part):
    return drawn_pair(key)[0].astype(jnp.bfloat16)


def draw_key_tokens(key, part):
    return drawn_pair(key)[1].astype(jnp.bfloat16)


def draw_values(key, part):
    common_key = jax.random.fold_in(key, 31)
    noise_key = jax.random.fold_in(key, 32)
    common = group_common(common_key)
    noise = jnp.clip(jax.random.normal(noise_key, (FRAMES, FTOK, HEADS * HD)), -4.0, 4.0)
    return (0.7 * common + 0.7 * noise).astype(jnp.bfloat16)


def near_tables(key):
    total_blocks = 3 * BLOCKS
    score_key = jax.random.fold_in(key, 21)
    count_key = jax.random.fold_in(key, 22)
    limit_key = jax.random.fold_in(key, 23)
    pick_key = jax.random.fold_in(key, 24)
    frame_ids = jnp.arange(FRAMES, dtype=jnp.int32)[:, None, None]
    query_blocks = jnp.arange(BLOCKS, dtype=jnp.int32)[None, :, None]
    key_blocks = jnp.arange(total_blocks, dtype=jnp.int32)[None, None, :]
    source = frame_ids + key_blocks // BLOCKS - 1
    usable = (source >= 0) & (source < FRAMES)
    own_block = key_blocks == BLOCKS + query_blocks
    scores = jax.random.randint(score_key, (FRAMES, BLOCKS, total_blocks), 0, 4096) * 256 + key_blocks
    scores = jnp.where(own_block, 8388608, jnp.where(usable, scores, -1 - key_blocks))
    top_scores, block_ids = lax.top_k(scores, LIST)
    limits = jax.random.randint(limit_key, (FRAMES, 1), 1, LIST + 1)
    counts = jax.random.randint(count_key, (FRAMES, BLOCKS), 0, 1048576) % limits + 1
    picked = jax.random.randint(pick_key, (), 0, FRAMES * BLOCKS)
    flat_ids = jnp.arange(FRAMES * BLOCKS, dtype=jnp.int32).reshape(FRAMES, BLOCKS)
    counts = jnp.where(flat_ids == picked, LIST, counts)
    return (block_ids.astype(jnp.int32), counts.astype(jnp.int32))


def draw_near_list(key, part):
    return near_tables(key)[0]


def draw_near_count(key, part):
    return near_tables(key)[1]


def draw_dist_band(key, part):
    cut_points = jax.random.randint(jax.random.fold_in(key, 41), (NBANDS - 1,), 2, FRAMES - 1)
    distance = jnp.arange(FRAMES, dtype=jnp.int32)
    band_index = 1 + jnp.sum((distance[:, None] > cut_points[None, :]).astype(jnp.int32), axis=1)
    return jnp.where(distance < 2, 0, band_index).astype(jnp.int32)


def draw_band_factor(key, part):
    levels = jax.random.randint(jax.random.fold_in(key, 51), (NBANDS,), 0, 3)
    factor = jnp.where(levels == 0, 1, jnp.where(levels == 1, 2, 4))
    picked = jax.random.randint(jax.random.fold_in(key, 52), (), 0, NBANDS)
    factor = jnp.where(jnp.arange(NBANDS, dtype=jnp.int32) == picked, 4, factor)
    return factor.astype(jnp.int32)


def setup_inputs(seed: int = 0) -> dict:
    seeds = jax.random.split(jax.random.key(seed), 8)
    queries = draw_queries(jax.random.fold_in(seeds[7], 71), 0)
    key_tokens = draw_key_tokens(jax.random.fold_in(seeds[7], 71), 0)
    values = draw_values(jax.random.fold_in(seeds[7], 71), 0)
    near_list = draw_near_list(jax.random.fold_in(seeds[7], 71), 0)
    near_count = draw_near_count(jax.random.fold_in(seeds[7], 71), 0)
    dist_band = draw_dist_band(jax.random.fold_in(seeds[7], 71), 0)
    band_factor = draw_band_factor(jax.random.fold_in(seeds[7], 71), 0)
    return {"queries": queries, "key_tokens": key_tokens, "values": values, "near_list": near_list, "near_count": near_count, "dist_band": dist_band, "band_factor": band_factor}


lowest_score = -1e+30

def lookup(table_values, positions):
    slot_ids = jnp.arange(table_values.shape[0], dtype=jnp.int32)
    picked = jnp.where(positions[:, None] == slot_ids[None, :], table_values[None, :], 0)
    return lax.optimization_barrier(jnp.sum(picked, axis=1)).astype(jnp.int32)

def coarsen(pooled, factor):
    frame_count, far_rows, head_count, head_size = pooled.shape
    widened = pooled.astype(jnp.float32)
    pair_means = lax.optimization_barrier(jnp.mean(widened.reshape(frame_count, far_rows // 2, 2, head_count, head_size), axis=2)).astype(jnp.bfloat16)
    quad_means = lax.optimization_barrier(jnp.mean(widened.reshape(frame_count, far_rows // 4, 4, head_count, head_size), axis=2)).astype(jnp.bfloat16)
    pair_means = jnp.repeat(pair_means, 2, axis=1)
    quad_means = jnp.repeat(quad_means, 4, axis=1)
    choose_factor = factor[:, None, None, None]
    return jnp.where(choose_factor == 1, pooled, jnp.where(choose_factor == 2, pair_means, quad_means))

def attend_block(query_rows, near_k, near_v, near_ok, far_k, far_v, far_bias, far_ok):
    score_scale = 1.0 / math.sqrt(query_rows.shape[-1])
    widened = query_rows.astype(jnp.float32)
    near_scores = jnp.einsum('bhd,khd->hbk', widened, near_k.astype(jnp.float32)) * score_scale
    far_scores = jnp.einsum('bhd,khd->hbk', widened, far_k.astype(jnp.float32)) * score_scale + far_bias[None, None, :]
    near_scores = jnp.where(near_ok[None, None, :], near_scores, lowest_score)
    far_scores = jnp.where(far_ok[None, None, :], far_scores, lowest_score)
    row_top = jnp.maximum(lax.optimization_barrier(jnp.max(near_scores, axis=-1, keepdims=True)), lax.optimization_barrier(jnp.max(far_scores, axis=-1, keepdims=True)))
    near_weights = jnp.where(near_ok[None, None, :], jnp.exp(near_scores - row_top), 0.0)
    far_weights = jnp.where(far_ok[None, None, :], jnp.exp(far_scores - row_top), 0.0)
    denominator = lax.optimization_barrier(jnp.sum(near_weights, axis=-1)) + lax.optimization_barrier(jnp.sum(far_weights, axis=-1))
    near_low = lax.optimization_barrier(near_weights.astype(jnp.bfloat16))
    far_low = lax.optimization_barrier(far_weights.astype(jnp.bfloat16))
    weighted = jnp.einsum('hbk,khd->bhd', near_low.astype(jnp.float32), near_v.astype(jnp.float32))
    weighted = weighted + jnp.einsum('hbk,khd->bhd', far_low.astype(jnp.float32), far_v.astype(jnp.float32))
    return (weighted / jnp.transpose(denominator)[:, :, None]).astype(jnp.bfloat16)

def attend_frame(query_frame, key_rim, value_rim, pooled_k, pooled_v, lists, counts, dist_band, band_factor, frame_index):
    frame_tokens, head_count, head_size = query_frame.shape
    block_count, list_length = lists.shape
    block_rows = frame_tokens // block_count
    frame_count, far_rows = (pooled_k.shape[0], pooled_k.shape[1])
    distance = jnp.abs(jnp.arange(frame_count, dtype=jnp.int32) - frame_index)
    band_index = lookup(dist_band, distance)
    factor = jnp.maximum(lookup(band_factor, band_index - 1), 1)
    far_k = lax.optimization_barrier(coarsen(pooled_k, factor)).reshape(frame_count * far_rows, head_count, head_size)
    far_v = lax.optimization_barrier(coarsen(pooled_v, factor)).reshape(frame_count * far_rows, head_count, head_size)
    far_bias = jnp.repeat(-jnp.log(factor.astype(jnp.float32)), far_rows)
    far_ok = jnp.repeat(distance >= 2, far_rows)
    key_blocks = key_rim.reshape(3 * block_count, block_rows, head_count, head_size)
    value_blocks = value_rim.reshape(3 * block_count, block_rows, head_count, head_size)

    def one_block(block_index):
        block_ids = lax.dynamic_index_in_dim(lists, block_index, 0, keepdims=False)
        live_slots = lax.dynamic_index_in_dim(counts, block_index, 0, keepdims=False)
        near_k = jnp.take(key_blocks, block_ids, axis=0).reshape(list_length * block_rows, head_count, head_size)
        near_v = jnp.take(value_blocks, block_ids, axis=0).reshape(list_length * block_rows, head_count, head_size)
        near_ok = jnp.repeat(jnp.arange(list_length, dtype=jnp.int32) < live_slots, block_rows)
        query_rows = lax.dynamic_slice_in_dim(query_frame, block_index * block_rows, block_rows, 0)
        return attend_block(query_rows, near_k, near_v, near_ok, far_k, far_v, far_bias, far_ok)
    results = lax.map(one_block, jnp.arange(block_count, dtype=jnp.int32))
    return results.reshape(frame_tokens, head_count, head_size)

def reference(queries, key_tokens, values, near_list, near_count, dist_band, band_factor):
    frame_count, frame_tokens, features = queries.shape
    head_count = features // HD
    query_heads = queries.reshape(frame_count, frame_tokens, head_count, HD)
    key_heads = key_tokens.reshape(frame_count, frame_tokens, head_count, HD)
    value_heads = values.reshape(frame_count, frame_tokens, head_count, HD)
    pooled_k = lax.optimization_barrier(jnp.mean(key_heads.reshape(frame_count, frame_tokens // POOL, POOL, head_count, HD), axis=2, dtype=jnp.float32)).astype(jnp.bfloat16)
    pooled_v = lax.optimization_barrier(jnp.mean(value_heads.reshape(frame_count, frame_tokens // POOL, POOL, head_count, HD), axis=2, dtype=jnp.float32)).astype(jnp.bfloat16)
    pooled_k = lax.optimization_barrier(pooled_k)
    pooled_v = lax.optimization_barrier(pooled_v)
    zero_frame = jnp.zeros((1, frame_tokens, head_count, HD), key_heads.dtype)
    key_padded = jnp.concatenate([zero_frame, key_heads, zero_frame], axis=0)
    value_padded = jnp.concatenate([zero_frame, value_heads, zero_frame], axis=0)

    def one_frame(frame_index):
        key_rim = lax.dynamic_slice_in_dim(key_padded, frame_index, 3, 0)
        value_rim = lax.dynamic_slice_in_dim(value_padded, frame_index, 3, 0)
        query_frame = lax.dynamic_index_in_dim(query_heads, frame_index, 0, keepdims=False)
        lists = lax.dynamic_index_in_dim(near_list, frame_index, 0, keepdims=False)
        counts = lax.dynamic_index_in_dim(near_count, frame_index, 0, keepdims=False)
        return attend_frame(query_frame, key_rim, value_rim, pooled_k, pooled_v, lists, counts, dist_band, band_factor, frame_index)
    results = lax.map(one_frame, jnp.arange(frame_count, dtype=jnp.int32))
    return results.reshape(frame_count, frame_tokens, features)
```

```python
import functools
import math

import jax
import jax.numpy as jnp
from jax import lax
from jax.experimental import pallas as pl
from jax.experimental.pallas import tpu as pltpu
from jax.sharding import PartitionSpec as P

HD = 128
POOL = 128
LOWEST = -1e30
MESH = pl.DeviceIdType.MESH


def kernel(
    frames,
    parts,
    list_ref,
    count_ref,
    band_ref,
    factor_ref,
    q_ref,
    k_ref,
    v_ref,
    out_ref,
    q_buf,
    k_buf,
    v_buf,
    far_buf,
    far_k,
    far_v,
    far_bias,
    scores,
    staged,
    local_sem,
    swap_send,
    swap_recv,
    side_send,
    side_recv,
    pool_send,
    pool_recv,
    back_send,
    back_recv,
):
    frame = lax.axis_index("tm")
    part = lax.axis_index("space")
    rows = q_buf.shape[1]
    slots = list_ref.shape[2]
    far_rows = far_buf.shape[2]
    far_total = frames * far_rows

    def shifted(step):
        return lax.rem(part + step, parts)

    def columns(index):
        return pl.ds(pl.multiple_of(index * HD, HD), HD)

    barrier = pltpu.get_barrier_semaphore()
    for step in range(1, parts):
        pl.semaphore_signal(
            barrier, inc=1, device_id=(frame, shifted(step)), device_id_type=MESH
        )
    for step in range(1, frames):
        pl.semaphore_signal(
            barrier,
            inc=1,
            device_id=(lax.rem(frame + step, frames), part),
            device_id_type=MESH,
        )
    pl.semaphore_wait(barrier, parts - 1 + frames - 1)

    sources = (k_ref, v_ref, q_ref)

    def landing(which, index):
        if which == 2:
            return q_buf.at[index]
        return (k_buf, v_buf)[which].at[parts + index]

    def swap(which, target, slot):
        return pltpu.make_async_remote_copy(
            src_ref=sources[which].at[:, columns(target)],
            dst_ref=landing(which, slot),
            send_sem=swap_send.at[which, target],
            recv_sem=swap_recv.at[which, slot],
            device_id=(frame, target),
            device_id_type=MESH,
        )

    def side(which, direction, index):
        there = index if direction == 0 else 2 * parts + index
        buf = (k_buf, v_buf)[which]
        target = frame + 1 if direction == 0 else frame - 1
        return pltpu.make_async_remote_copy(
            src_ref=buf.at[parts + index],
            dst_ref=buf.at[there],
            send_sem=side_send.at[direction, which, index],
            recv_sem=side_recv.at[direction, which, index],
            device_id=(target, part),
            device_id_type=MESH,
        )

    own = [
        pltpu.make_async_copy(
            sources[which].at[:, columns(part)], landing(which, part), local_sem.at[which]
        )
        for which in range(3)
    ]
    for copy in own:
        copy.start()
    for which in range(3):
        for step in range(1, parts):
            swap(which, shifted(step), part).start()

    def forward(which, index):
        @pl.when(frame < frames - 1)
        def _():
            side(which, 0, index).start()

        @pl.when(frame > 0)
        def _():
            side(which, 1, index).start()

    own[0].wait()
    forward(0, part)
    own[1].wait()
    forward(1, part)
    for which in range(2):
        for step in range(1, parts):
            source = shifted(step)
            swap(which, source, source).wait_recv()
            forward(which, source)

    tokens = parts * rows
    pool_row = lax.broadcasted_iota(jnp.int32, (far_rows, tokens), 0)
    pool_col = lax.broadcasted_iota(jnp.int32, (far_rows, tokens), 1)
    average = jnp.where(pool_row == pool_col // POOL, 1.0 / POOL, 0.0).astype(jnp.bfloat16)
    for which, buf in enumerate((k_buf, v_buf)):
        frame_rows = buf[parts : 2 * parts].reshape(tokens, HD)
        pooled = jnp.dot(average, frame_rows, preferred_element_type=jnp.float32)
        far_buf[frame, which] = pooled.astype(jnp.bfloat16).astype(jnp.float32)

    def share(target, slot):
        return pltpu.make_async_remote_copy(
            src_ref=far_buf.at[slot],
            dst_ref=far_buf.at[slot],
            send_sem=pool_send.at[target],
            recv_sem=pool_recv.at[slot],
            device_id=(target, part),
            device_id_type=MESH,
        )

    for step in range(1, frames):
        share(lax.rem(frame + step, frames), frame).start()

    own[2].wait()
    for step in range(1, parts):
        source = shifted(step)
        swap(2, source, source).wait_recv()
    for step in range(1, frames):
        source = lax.rem(frame + step, frames)
        share(source, source).wait_recv()

    mix_row = lax.broadcasted_iota(jnp.int32, (far_total, far_total), 0)
    mix_col = lax.broadcasted_iota(jnp.int32, (far_total, far_total), 1)
    lane_frame = lax.broadcasted_iota(jnp.int32, (8, far_total), 1) // far_rows
    row_frame = mix_row // far_rows
    factor_rows = jnp.ones((far_total, far_total), jnp.int32)
    bias = jnp.full((8, far_total), LOWEST, jnp.float32)
    for other in range(frames):
        distance = jnp.abs(frame - other)
        band = band_ref[distance]
        factor = jnp.int32(1)
        for entry in range(factor_ref.shape[0]):
            factor = jnp.where(band == entry + 1, factor_ref[entry], factor)
        offset = jnp.where(
            factor == 1,
            jnp.float32(0.0),
            jnp.where(factor == 2, jnp.float32(-math.log(2.0)), jnp.float32(-math.log(4.0))),
        )
        offset = jnp.where(distance >= 2, offset, jnp.float32(LOWEST))
        factor_rows = jnp.where(row_frame == other, factor, factor_rows)
        bias = jnp.where(lane_frame == other, offset, bias)
    mix = jnp.where(
        factor_rows == 1,
        jnp.where(mix_row == mix_col, 1.0, 0.0),
        jnp.where(
            factor_rows == 2,
            jnp.where(mix_row // 2 == mix_col // 2, 0.5, 0.0),
            jnp.where(mix_row // 4 == mix_col // 4, 0.25, 0.0),
        ),
    ).astype(jnp.bfloat16)
    far_bias[...] = bias
    for which, far in enumerate((far_k, far_v)):
        pooled = far_buf[:, which].reshape(far_total, HD).astype(jnp.bfloat16)
        far[...] = jnp.dot(mix, pooled, preferred_element_type=jnp.float32).astype(jnp.bfloat16)

    for which in range(2):
        for index in range(parts):

            @pl.when(frame > 0)
            def _(which=which, index=index):
                arrived = (k_buf, v_buf)[which].at[index]
                pltpu.make_async_remote_copy(
                    src_ref=arrived,
                    dst_ref=arrived,
                    send_sem=side_send.at[0, which, index],
                    recv_sem=side_recv.at[0, which, index],
                    device_id=(frame - 1, part),
                    device_id_type=MESH,
                ).wait_recv()

            @pl.when(frame < frames - 1)
            def _(which=which, index=index):
                arrived = (k_buf, v_buf)[which].at[2 * parts + index]
                pltpu.make_async_remote_copy(
                    src_ref=arrived,
                    dst_ref=arrived,
                    send_sem=side_send.at[1, which, index],
                    recv_sem=side_recv.at[1, which, index],
                    device_id=(frame + 1, part),
                    device_id_type=MESH,
                ).wait_recv()

    scale = 1.0 / math.sqrt(HD)
    contract = (((1,), (1,)), ((), ()))

    def attend(block):
        query = q_buf[block]
        live = count_ref[frame, block]
        near_wide = slots * rows
        far_scores = (
            lax.dot_general(query, far_k[...], contract, preferred_element_type=jnp.float32)
            * scale
            + far_bias[0:1, :]
        )
        top = jnp.max(far_scores, axis=1, keepdims=True)
        for slot in range(slots):
            keys = k_buf[list_ref[frame, block, slot]]
            hidden = jnp.where(slot < live, jnp.float32(0.0), jnp.float32(LOWEST))
            part_scores = (
                lax.dot_general(query, keys, contract, preferred_element_type=jnp.float32) * scale
                + hidden
            )
            scores[:, slot * rows : (slot + 1) * rows] = part_scores
            top = jnp.maximum(top, jnp.max(part_scores, axis=1, keepdims=True))
        weights = jnp.exp(far_scores - top)
        total = jnp.sum(weights, axis=1, keepdims=True)
        summed = jnp.dot(
            weights.astype(jnp.bfloat16), far_v[...], preferred_element_type=jnp.float32
        )
        for slot in range(slots):
            near_values = v_buf[list_ref[frame, block, slot]]
            weights = jnp.exp(scores[:, slot * rows : (slot + 1) * rows] - top)
            total = total + jnp.sum(weights, axis=1, keepdims=True)
            summed = summed + jnp.dot(
                weights.astype(jnp.bfloat16), near_values, preferred_element_type=jnp.float32
            )
        return (summed / total).astype(jnp.bfloat16)

    def back(target, slot):
        return pltpu.make_async_remote_copy(
            src_ref=staged.at[target],
            dst_ref=out_ref.at[:, columns(slot)],
            send_sem=back_send.at[target],
            recv_sem=back_recv.at[slot],
            device_id=(frame, target),
            device_id_type=MESH,
        )

    def one(step, carry):
        target = lax.rem(part + step, parts)
        staged[target] = attend(target)
        back(target, part).start()
        return carry

    lax.fori_loop(1, parts, one, 0)
    out_ref[:, columns(part)] = attend(part)

    for step in range(1, parts):
        other = shifted(step)
        back(other, other).wait_recv()
        back(other, part).wait_send()
        for which in range(3):
            swap(which, other, part).wait_send()
    for step in range(1, frames):
        share(lax.rem(frame + step, frames), frame).wait_send()
    for which in range(2):
        for index in range(parts):

            @pl.when(frame < frames - 1)
            def _(which=which, index=index):
                side(which, 0, index).wait_send()

            @pl.when(frame > 0)
            def _(which=which, index=index):
                side(which, 1, index).wait_send()


def local(frames, parts, queries, key_tokens, values, near_list, near_count, dist_band, band_factor):
    _, rows, features = queries.shape
    far_rows = parts * rows // POOL
    far_total = frames * far_rows
    slots = near_list.shape[2]
    smem = pl.BlockSpec(memory_space=pltpu.SMEM)
    anywhere = pl.BlockSpec(memory_space=pl.ANY)
    dma = pltpu.SemaphoreType.DMA
    out = pl.pallas_call(
        functools.partial(kernel, frames, parts),
        out_shape=jax.ShapeDtypeStruct((rows, features), jnp.bfloat16),
        in_specs=[smem] * 4 + [anywhere] * 3,
        out_specs=pl.BlockSpec(memory_space=pltpu.VMEM),
        scratch_shapes=[
            pltpu.VMEM((parts, rows, HD), jnp.bfloat16),
            pltpu.VMEM((3 * parts, rows, HD), jnp.bfloat16),
            pltpu.VMEM((3 * parts, rows, HD), jnp.bfloat16),
            pltpu.VMEM((frames, 2, far_rows, HD), jnp.float32),
            pltpu.VMEM((far_total, HD), jnp.bfloat16),
            pltpu.VMEM((far_total, HD), jnp.bfloat16),
            pltpu.VMEM((8, far_total), jnp.float32),
            pltpu.VMEM((rows, slots * rows), jnp.float32),
            pltpu.VMEM((parts, rows, HD), jnp.bfloat16),
            dma((3,)),
            dma((3, parts)),
            dma((3, parts)),
            dma((2, 2, parts)),
            dma((2, 2, parts)),
            dma((frames,)),
            dma((frames,)),
            dma((parts,)),
            dma((parts,)),
        ],
        compiler_params=pltpu.CompilerParams(
            collective_id=0, has_side_effects=True, vmem_limit_bytes=40 * 2**20
        ),
        cost_estimate=pl.CostEstimate(
            flops=4 * parts * rows * (slots * rows + far_total) * HD,
            bytes_accessed=8 * rows * features,
            transcendentals=parts * rows * (slots * rows + far_total),
        ),
    )(
        near_list,
        near_count,
        dist_band,
        band_factor,
        queries[0],
        key_tokens[0],
        values[0],
    )
    return out[None]


def solution(mesh):
    return jax.shard_map(
        functools.partial(local, mesh.shape["tm"], mesh.shape["space"]),
        mesh=mesh,
        in_specs=(
            P("tm", "space", None),
            P("tm", "space", None),
            P("tm", "space", None),
            P(),
            P(),
            P(),
            P(),
        ),
        out_specs=P("tm", "space", None),
        check_vma=False,
    )
```

```python
import functools
import math

import jax
import jax.numpy as jnp
from jax import lax
from jax.experimental import pallas as pl
from jax.experimental.pallas import tpu as pltpu
from jax.sharding import PartitionSpec as P

HD = 128
POOL = 128
LOWEST = -1e30
MESH = pl.DeviceIdType.MESH


def kernel(
    frames,
    parts,
    list_ref,
    count_ref,
    band_ref,
    factor_ref,
    q_ref,
    k_ref,
    v_ref,
    out_ref,
    k_rows,
    v_rows,
    q_buf,
    k_buf,
    v_buf,
    pool_out,
    far_buf,
    far_k,
    far_v,
    far_bias,
    scores,
    near_weights,
    far_weights,
    totals,
    staged,
    local_sem,
    swap_send,
    swap_recv,
    side_send,
    side_recv,
    part_send,
    part_recv,
    pool_send,
    pool_recv,
    back_send,
    back_recv,
):
    frame = lax.axis_index("tm")
    part = lax.axis_index("space")
    rows = q_buf.shape[1]
    slots = list_ref.shape[2]
    each = rows // POOL
    far_rows = parts * each
    far_total = frames * far_rows
    steps = [(parts // 2 - 1 + i) % (parts - 1) + 1 for i in range(parts - 1)]

    def shifted(step):
        return lax.rem(part + step, parts)

    def columns(index):
        return pl.ds(pl.multiple_of(index * HD, HD), HD)

    sources = (k_ref, v_ref, q_ref)

    def landing(which, index):
        if which == 2:
            return q_buf.at[index]
        return (k_buf, v_buf)[which].at[parts + index]

    whole = [
        pltpu.make_async_copy(k_ref, k_rows, local_sem.at[3]),
        pltpu.make_async_copy(v_ref, v_rows, local_sem.at[4]),
    ]
    own = [
        pltpu.make_async_copy(
            sources[which].at[:, columns(part)], landing(which, part), local_sem.at[which]
        )
        for which in range(3)
    ]
    for copy in whole + own:
        copy.start()

    barrier = pltpu.get_barrier_semaphore()
    for step in range(1, parts):
        pl.semaphore_signal(
            barrier, inc=1, device_id=(frame, shifted(step)), device_id_type=MESH
        )
    for step in range(1, frames):
        pl.semaphore_signal(
            barrier,
            inc=1,
            device_id=(lax.rem(frame + step, frames), part),
            device_id_type=MESH,
        )
    pl.semaphore_wait(barrier, parts - 1 + frames - 1)

    def swap(which, target, slot):
        return pltpu.make_async_remote_copy(
            src_ref=sources[which].at[:, columns(target)],
            dst_ref=landing(which, slot),
            send_sem=swap_send.at[which, target],
            recv_sem=swap_recv.at[which, slot],
            device_id=(frame, target),
            device_id_type=MESH,
        )

    def side(which, direction, index):
        there = index if direction == 0 else 2 * parts + index
        buf = (k_buf, v_buf)[which]
        target = frame + 1 if direction == 0 else frame - 1
        return pltpu.make_async_remote_copy(
            src_ref=buf.at[parts + index],
            dst_ref=buf.at[there],
            send_sem=side_send.at[direction, which, index],
            recv_sem=side_recv.at[direction, which, index],
            device_id=(target, part),
            device_id_type=MESH,
        )

    def forward(which, index):
        @pl.when(frame < frames - 1)
        def _():
            side(which, 0, index).start()

        @pl.when(frame > 0)
        def _():
            side(which, 1, index).start()

    def arrivals(which):
        for index in range(parts):

            @pl.when(frame > 0)
            def _(index=index):
                arrived = (k_buf, v_buf)[which].at[index]
                pltpu.make_async_remote_copy(
                    src_ref=arrived,
                    dst_ref=arrived,
                    send_sem=side_send.at[0, which, index],
                    recv_sem=side_recv.at[0, which, index],
                    device_id=(frame - 1, part),
                    device_id_type=MESH,
                ).wait_recv()

            @pl.when(frame < frames - 1)
            def _(index=index):
                arrived = (k_buf, v_buf)[which].at[2 * parts + index]
                pltpu.make_async_remote_copy(
                    src_ref=arrived,
                    dst_ref=arrived,
                    send_sem=side_send.at[1, which, index],
                    recv_sem=side_recv.at[1, which, index],
                    device_id=(frame + 1, part),
                    device_id_type=MESH,
                ).wait_recv()

    def spread(target, slot):
        return pltpu.make_async_remote_copy(
            src_ref=pool_out.at[:, columns(target)],
            dst_ref=far_buf.at[frame, slot],
            send_sem=part_send.at[target],
            recv_sem=part_recv.at[slot],
            device_id=(frame, target),
            device_id_type=MESH,
        )

    def share(target, slot):
        return pltpu.make_async_remote_copy(
            src_ref=far_buf.at[slot],
            dst_ref=far_buf.at[slot],
            send_sem=pool_send.at[target],
            recv_sem=pool_recv.at[slot],
            device_id=(target, part),
            device_id_type=MESH,
        )

    for step in steps:
        swap(0, shifted(step), part).start()

    pool_row = lax.broadcasted_iota(jnp.int32, (8, rows), 0)
    pool_col = lax.broadcasted_iota(jnp.int32, (8, rows), 1) // POOL
    pooled = jnp.zeros((8, k_rows.shape[1]), jnp.float32)
    for which, taken in enumerate((k_rows, v_rows)):
        whole[which].wait()
        average = jnp.where(pool_row == pool_col + which * each, 1.0 / POOL, 0.0)
        pooled = pooled + jnp.dot(
            average.astype(jnp.bfloat16), taken[...], preferred_element_type=jnp.float32
        )
    pool_out[...] = pooled.astype(jnp.bfloat16).astype(jnp.float32)
    far_buf[frame, part] = pool_out[:, columns(part)]
    for step in steps:
        spread(shifted(step), part).start()

    for which in (2, 1):
        for step in steps:
            swap(which, shifted(step), part).start()

    for which in range(2):
        own[which].wait()
        forward(which, part)
    for step in steps:
        source = shifted(parts - step)
        swap(0, source, source).wait_recv()
        forward(0, source)
    for step in steps:
        source = shifted(parts - step)
        spread(source, source).wait_recv()
    for step in range(1, frames):
        share(lax.rem(frame + step, frames), frame).start()
    for step in range(1, frames):
        source = lax.rem(frame + step, frames)
        share(source, source).wait_recv()

    mix_row = lax.broadcasted_iota(jnp.int32, (far_rows, parts * 8), 0)
    mix_col = lax.broadcasted_iota(jnp.int32, (far_rows, parts * 8), 1)
    lane_frame = lax.broadcasted_iota(jnp.int32, (8, far_total), 1) // far_rows
    mixes = []
    for which in range(2):
        inner = mix_col % 8 - which * each
        held = (inner >= 0) & (inner < each)
        index = (mix_col // 8) * each + inner
        mixes.append(
            [
                jnp.where(held & (mix_row // e == index // e), 1.0 / e, 0.0)
                for e in (1, 2, 4)
            ]
        )
    bias = jnp.full((8, far_total), LOWEST, jnp.float32)
    for other in range(frames):
        distance = jnp.abs(frame - other)
        band = band_ref[distance]
        factor = jnp.int32(1)
        for entry in range(factor_ref.shape[0]):
            factor = jnp.where(band == entry + 1, factor_ref[entry], factor)
        offset = jnp.where(
            factor == 1,
            jnp.float32(0.0),
            jnp.where(factor == 2, jnp.float32(-math.log(2.0)), jnp.float32(-math.log(4.0))),
        )
        offset = jnp.where(distance >= 2, offset, jnp.float32(LOWEST))
        bias = jnp.where(lane_frame == other, offset, bias)
        pooled = far_buf[other].reshape(parts * 8, HD).astype(jnp.bfloat16)
        for which, far in enumerate((far_k, far_v)):
            once, pairs, quads = mixes[which]
            mix = jnp.where(factor == 1, once, jnp.where(factor == 2, pairs, quads))
            coarse = jnp.dot(
                mix.astype(jnp.bfloat16), pooled, preferred_element_type=jnp.float32
            )
            far[other] = coarse.astype(jnp.bfloat16).astype(jnp.float32)
    far_bias[...] = bias

    own[2].wait()
    for step in steps:
        source = shifted(parts - step)
        swap(2, source, source).wait_recv()
    arrivals(0)

    scale = 1.0 / math.sqrt(HD)
    contract = (((1,), (1,)), ((), ()))

    def weigh(block, carry):
        query = q_buf[block]
        live = count_ref[block, frame]
        far_scores = (
            lax.dot_general(
                query,
                far_k[...].reshape(far_total, HD).astype(jnp.bfloat16),
                contract,
                preferred_element_type=jnp.float32,
            )
            * scale
            + far_bias[0:1, :]
        )
        top = jnp.max(far_scores, axis=1, keepdims=True)
        for slot in range(slots):
            keys = k_buf[list_ref[frame, block, slot]]
            hidden = jnp.where(slot < live, jnp.float32(0.0), jnp.float32(LOWEST))
            near_scores = (
                lax.dot_general(query, keys, contract, preferred_element_type=jnp.float32) * scale
                + hidden
            )
            scores[:, slot * rows : (slot + 1) * rows] = near_scores
            top = jnp.maximum(top, jnp.max(near_scores, axis=1, keepdims=True))
        weights = jnp.exp(far_scores - top)
        total = jnp.sum(weights, axis=1, keepdims=True)
        far_weights[block] = weights.astype(jnp.bfloat16)
        for slot in range(slots):
            span = slice(slot * rows, (slot + 1) * rows)
            weights = jnp.exp(scores[:, span] - top)
            total = total + jnp.sum(weights, axis=1, keepdims=True)
            near_weights[block, :, span] = weights.astype(jnp.bfloat16)
        totals[block] = jnp.broadcast_to(total, (rows, HD))
        return carry

    lax.fori_loop(0, parts, weigh, 0)

    for step in steps:
        source = shifted(parts - step)
        swap(1, source, source).wait_recv()
        forward(1, source)
    arrivals(1)

    def attend(block):
        summed = jnp.dot(
            far_weights[block],
            far_v[...].reshape(far_total, HD).astype(jnp.bfloat16),
            preferred_element_type=jnp.float32,
        )
        for slot in range(slots):
            summed = summed + jnp.dot(
                near_weights[block, :, slot * rows : (slot + 1) * rows],
                v_buf[list_ref[frame, block, slot]],
                preferred_element_type=jnp.float32,
            )
        return (summed / totals[block]).astype(jnp.bfloat16)

    def back(target, slot):
        return pltpu.make_async_remote_copy(
            src_ref=staged.at[target],
            dst_ref=out_ref.at[:, columns(slot)],
            send_sem=back_send.at[target],
            recv_sem=back_recv.at[slot],
            device_id=(frame, target),
            device_id_type=MESH,
        )

    def one(i, carry):
        target = shifted((parts // 2 - 1 + i) % (parts - 1) + 1)
        staged[target] = attend(target)
        back(target, part).start()
        return carry

    lax.fori_loop(0, parts - 1, one, 0)
    out_ref[:, columns(part)] = attend(part)

    for step in steps:
        other = shifted(step)
        back(other, other).wait_recv()
        back(other, part).wait_send()
        spread(other, part).wait_send()
        for which in range(3):
            swap(which, other, part).wait_send()
    for step in range(1, frames):
        share(lax.rem(frame + step, frames), frame).wait_send()
    for which in range(2):
        for index in range(parts):

            @pl.when(frame < frames - 1)
            def _(which=which, index=index):
                side(which, 0, index).wait_send()

            @pl.when(frame > 0)
            def _(which=which, index=index):
                side(which, 1, index).wait_send()


def local(frames, parts, queries, key_tokens, values, near_list, near_count, dist_band, band_factor):
    _, rows, features = queries.shape
    far_rows = parts * rows // POOL
    far_total = frames * far_rows
    slots = near_list.shape[2]
    smem = pl.BlockSpec(memory_space=pltpu.SMEM)
    anywhere = pl.BlockSpec(memory_space=pl.ANY)
    dma = pltpu.SemaphoreType.DMA
    out = pl.pallas_call(
        functools.partial(kernel, frames, parts),
        out_shape=jax.ShapeDtypeStruct((rows, features), jnp.bfloat16),
        in_specs=[smem] * 4 + [anywhere] * 3,
        out_specs=pl.BlockSpec(memory_space=pltpu.VMEM),
        scratch_shapes=[
            pltpu.VMEM((rows, features), jnp.bfloat16),
            pltpu.VMEM((rows, features), jnp.bfloat16),
            pltpu.VMEM((parts, rows, HD), jnp.bfloat16),
            pltpu.VMEM((3 * parts, rows, HD), jnp.bfloat16),
            pltpu.VMEM((3 * parts, rows, HD), jnp.bfloat16),
            pltpu.VMEM((8, features), jnp.float32),
            pltpu.VMEM((frames, parts, 8, HD), jnp.float32),
            pltpu.VMEM((frames, far_rows, HD), jnp.float32),
            pltpu.VMEM((frames, far_rows, HD), jnp.float32),
            pltpu.VMEM((8, far_total), jnp.float32),
            pltpu.VMEM((rows, slots * rows), jnp.float32),
            pltpu.VMEM((parts, rows, slots * rows), jnp.bfloat16),
            pltpu.VMEM((parts, rows, far_total), jnp.bfloat16),
            pltpu.VMEM((parts, rows, HD), jnp.float32),
            pltpu.VMEM((parts, rows, HD), jnp.bfloat16),
            dma((5,)),
            dma((3, parts)),
            dma((3, parts)),
            dma((2, 2, parts)),
            dma((2, 2, parts)),
            dma((parts,)),
            dma((parts,)),
            dma((frames,)),
            dma((frames,)),
            dma((parts,)),
            dma((parts,)),
        ],
        compiler_params=pltpu.CompilerParams(
            collective_id=0, has_side_effects=True, vmem_limit_bytes=62 * 2**20
        ),
        cost_estimate=pl.CostEstimate(
            flops=4 * parts * rows * (slots * rows + far_total) * HD,
            bytes_accessed=8 * rows * features,
            transcendentals=parts * rows * (slots * rows + far_total),
        ),
    )(
        near_list,
        near_count.T,
        dist_band,
        band_factor,
        queries[0],
        key_tokens[0],
        values[0],
    )
    return out[None]


def solution(mesh):
    return jax.shard_map(
        functools.partial(local, mesh.shape["tm"], mesh.shape["space"]),
        mesh=mesh,
        in_specs=(
            P("tm", "space", None),
            P("tm", "space", None),
            P("tm", "space", None),
            P(),
            P(),
            P(),
            P(),
        ),
        out_specs=P("tm", "space", None),
        check_vma=False,
    )
```

```python
import functools
import math

import jax
import jax.numpy as jnp
from jax import lax
from jax.experimental import pallas as pl
from jax.experimental.pallas import tpu as pltpu
from jax.sharding import PartitionSpec as P

HD = 128
POOL = 128
LOWEST = -1e30
MESH = pl.DeviceIdType.MESH


def kernel(
    frames,
    parts,
    list_ref,
    count_ref,
    band_ref,
    factor_ref,
    q_ref,
    k_ref,
    v_ref,
    out_ref,
    heads,
    q_buf,
    k_buf,
    v_buf,
    pool_out,
    far_buf,
    far_k,
    far_v,
    far_bias,
    scores,
    near_weights,
    far_weights,
    totals,
    staged,
    returned,
    local_sem,
    head_sem,
    swap_send,
    swap_recv,
    side_send,
    side_recv,
    part_send,
    part_recv,
    pool_send,
    pool_recv,
    back_send,
    back_recv,
):
    frame = lax.axis_index("tm")
    part = lax.axis_index("space")
    rows = q_buf.shape[1]
    slots = list_ref.shape[2]
    each = rows // POOL
    far_rows = parts * each
    far_total = frames * far_rows
    steps = [(parts // 2 - 1 + i) % (parts - 1) + 1 for i in range(parts - 1)]

    def shifted(step):
        return lax.rem(part + step, parts)

    def columns(index):
        return pl.ds(pl.multiple_of(index * HD, HD), HD)

    sources = (k_ref, v_ref, q_ref)

    def landing(which, index):
        if which == 2:
            return q_buf.at[index]
        return (k_buf, v_buf)[which].at[parts + index]

    split = [
        [
            pltpu.make_async_copy(
                sources[which].at[:, head * HD : (head + 1) * HD],
                heads.at[which, head],
                head_sem.at[which, head],
            )
            for head in range(parts)
        ]
        for which in range(3)
    ]
    own = [
        pltpu.make_async_copy(
            sources[which].at[:, columns(part)], landing(which, part), local_sem.at[which]
        )
        for which in range(3)
    ]
    for which in (0, 2, 1):
        for copy in split[which] + [own[which]]:
            copy.start()

    barrier = pltpu.get_barrier_semaphore()
    for step in range(1, parts):
        pl.semaphore_signal(
            barrier, inc=1, device_id=(frame, shifted(step)), device_id_type=MESH
        )
    for step in range(1, frames):
        pl.semaphore_signal(
            barrier,
            inc=1,
            device_id=(lax.rem(frame + step, frames), part),
            device_id_type=MESH,
        )
    pl.semaphore_wait(barrier, parts - 1 + frames - 1)

    def swap(which, target, slot):
        return pltpu.make_async_remote_copy(
            src_ref=heads.at[which, target],
            dst_ref=landing(which, slot),
            send_sem=swap_send.at[which, target],
            recv_sem=swap_recv.at[which, slot],
            device_id=(frame, target),
            device_id_type=MESH,
        )

    def side(which, direction, index):
        there = index if direction == 0 else 2 * parts + index
        buf = (k_buf, v_buf)[which]
        target = frame + 1 if direction == 0 else frame - 1
        return pltpu.make_async_remote_copy(
            src_ref=buf.at[parts + index],
            dst_ref=buf.at[there],
            send_sem=side_send.at[direction, which, index],
            recv_sem=side_recv.at[direction, which, index],
            device_id=(target, part),
            device_id_type=MESH,
        )

    def forward(which, index):
        @pl.when(frame < frames - 1)
        def _():
            side(which, 0, index).start()

        @pl.when(frame > 0)
        def _():
            side(which, 1, index).start()

    def arrivals(which):
        for index in range(parts):

            @pl.when(frame > 0)
            def _(index=index):
                arrived = (k_buf, v_buf)[which].at[index]
                pltpu.make_async_remote_copy(
                    src_ref=arrived,
                    dst_ref=arrived,
                    send_sem=side_send.at[0, which, index],
                    recv_sem=side_recv.at[0, which, index],
                    device_id=(frame - 1, part),
                    device_id_type=MESH,
                ).wait_recv()

            @pl.when(frame < frames - 1)
            def _(index=index):
                arrived = (k_buf, v_buf)[which].at[2 * parts + index]
                pltpu.make_async_remote_copy(
                    src_ref=arrived,
                    dst_ref=arrived,
                    send_sem=side_send.at[1, which, index],
                    recv_sem=side_recv.at[1, which, index],
                    device_id=(frame + 1, part),
                    device_id_type=MESH,
                ).wait_recv()

    def spread(target, slot):
        return pltpu.make_async_remote_copy(
            src_ref=pool_out.at[target],
            dst_ref=far_buf.at[frame, slot],
            send_sem=part_send.at[target],
            recv_sem=part_recv.at[slot],
            device_id=(frame, target),
            device_id_type=MESH,
        )

    def share(target, slot):
        return pltpu.make_async_remote_copy(
            src_ref=far_buf.at[slot],
            dst_ref=far_buf.at[slot],
            send_sem=pool_send.at[target],
            recv_sem=pool_recv.at[slot],
            device_id=(target, part),
            device_id_type=MESH,
        )

    for copy in split[0]:
        copy.wait()
    for step in steps:
        swap(0, shifted(step), part).start()
    for which in (2, 1):
        for copy in split[which]:
            copy.wait()

    pool_row = lax.broadcasted_iota(jnp.int32, (8, rows), 0)
    pool_col = lax.broadcasted_iota(jnp.int32, (8, rows), 1) // POOL
    averages = [
        jnp.where(pool_row == pool_col + which * each, 1.0 / POOL, 0.0).astype(jnp.bfloat16)
        for which in range(2)
    ]
    for head in range(parts):
        pooled = sum(
            jnp.dot(averages[which], heads[which, head], preferred_element_type=jnp.float32)
            for which in range(2)
        )
        pool_out[head] = pooled.astype(jnp.bfloat16).astype(jnp.float32)
    far_buf[frame, part] = pool_out[part]
    for step in steps:
        spread(shifted(step), part).start()

    for which in (1, 2):
        for step in steps:
            swap(which, shifted(step), part).start()

    for which in range(2):
        own[which].wait()
        forward(which, part)
    for step in steps:
        source = shifted(parts - step)
        swap(0, source, source).wait_recv()
        forward(0, source)
    for step in steps:
        source = shifted(parts - step)
        spread(source, source).wait_recv()
    for step in range(1, frames):
        share(lax.rem(frame + step, frames), frame).start()
    for step in steps:
        source = shifted(parts - step)
        swap(1, source, source).wait_recv()
        forward(1, source)
    for step in range(1, frames):
        source = lax.rem(frame + step, frames)
        share(source, source).wait_recv()

    mix_row = lax.broadcasted_iota(jnp.int32, (far_rows, parts * 8), 0)
    mix_col = lax.broadcasted_iota(jnp.int32, (far_rows, parts * 8), 1)
    lane_frame = lax.broadcasted_iota(jnp.int32, (8, far_total), 1) // far_rows
    mixes = []
    for which in range(2):
        inner = mix_col % 8 - which * each
        held = (inner >= 0) & (inner < each)
        index = (mix_col // 8) * each + inner
        mixes.append(
            [
                jnp.where(held & (mix_row // e == index // e), 1.0 / e, 0.0)
                for e in (1, 2, 4)
            ]
        )
    bias = jnp.full((8, far_total), LOWEST, jnp.float32)
    for other in range(frames):
        distance = jnp.abs(frame - other)
        band = band_ref[distance]
        factor = jnp.int32(1)
        for entry in range(factor_ref.shape[0]):
            factor = jnp.where(band == entry + 1, factor_ref[entry], factor)
        offset = jnp.where(
            factor == 1,
            jnp.float32(0.0),
            jnp.where(factor == 2, jnp.float32(-math.log(2.0)), jnp.float32(-math.log(4.0))),
        )
        offset = jnp.where(distance >= 2, offset, jnp.float32(LOWEST))
        bias = jnp.where(lane_frame == other, offset, bias)
        pooled = far_buf[other].reshape(parts * 8, HD).astype(jnp.bfloat16)
        for which, far in enumerate((far_k, far_v)):
            once, pairs, quads = mixes[which]
            mix = jnp.where(factor == 1, once, jnp.where(factor == 2, pairs, quads))
            coarse = jnp.dot(
                mix.astype(jnp.bfloat16), pooled, preferred_element_type=jnp.float32
            )
            far[other] = coarse.astype(jnp.bfloat16).astype(jnp.float32)
    far_bias[...] = bias

    own[2].wait()
    for step in steps:
        source = shifted(parts - step)
        swap(2, source, source).wait_recv()
    arrivals(0)

    scale = 1.0 / math.sqrt(HD)
    contract = (((1,), (1,)), ((), ()))

    def weigh(block, carry):
        query = q_buf[block]
        live = count_ref[block, frame]
        far_scores = (
            lax.dot_general(
                query,
                far_k[...].reshape(far_total, HD).astype(jnp.bfloat16),
                contract,
                preferred_element_type=jnp.float32,
            )
            * scale
            + far_bias[0:1, :]
        )
        top = jnp.max(far_scores, axis=1, keepdims=True)
        for slot in range(slots):
            keys = k_buf[list_ref[frame, block, slot]]
            hidden = jnp.where(slot < live, jnp.float32(0.0), jnp.float32(LOWEST))
            near_scores = (
                lax.dot_general(query, keys, contract, preferred_element_type=jnp.float32) * scale
                + hidden
            )
            scores[:, slot * rows : (slot + 1) * rows] = near_scores
            top = jnp.maximum(top, jnp.max(near_scores, axis=1, keepdims=True))
        weights = jnp.exp(far_scores - top)
        total = jnp.sum(weights, axis=1, keepdims=True)
        far_weights[block] = weights.astype(jnp.bfloat16)
        for slot in range(slots):
            span = slice(slot * rows, (slot + 1) * rows)
            weights = jnp.exp(scores[:, span] - top)
            total = total + jnp.sum(weights, axis=1, keepdims=True)
            near_weights[block, :, span] = weights.astype(jnp.bfloat16)
        totals[block] = jnp.broadcast_to(total, (rows, HD))
        return carry

    lax.fori_loop(0, parts, weigh, 0)

    arrivals(1)

    def attend(block):
        summed = jnp.dot(
            far_weights[block],
            far_v[...].reshape(far_total, HD).astype(jnp.bfloat16),
            preferred_element_type=jnp.float32,
        )
        for slot in range(slots):
            summed = summed + jnp.dot(
                near_weights[block, :, slot * rows : (slot + 1) * rows],
                v_buf[list_ref[frame, block, slot]],
                preferred_element_type=jnp.float32,
            )
        return (summed / totals[block]).astype(jnp.bfloat16)

    def back(target, slot):
        return pltpu.make_async_remote_copy(
            src_ref=staged.at[target],
            dst_ref=returned.at[slot],
            send_sem=back_send.at[target],
            recv_sem=back_recv.at[slot],
            device_id=(frame, target),
            device_id_type=MESH,
        )

    def one(i, carry):
        target = shifted((parts // 2 - 1 + i) % (parts - 1) + 1)
        staged[target] = attend(target)
        back(target, part).start()
        return carry

    lax.fori_loop(0, parts - 1, one, 0)
    returned[part] = attend(part)

    for step in steps:
        other = shifted(step)
        back(other, other).wait_recv()
    for head in range(parts):
        out_ref[:, head * HD : (head + 1) * HD] = returned[head]
    for step in steps:
        other = shifted(step)
        back(other, part).wait_send()
        spread(other, part).wait_send()
        for which in range(3):
            swap(which, other, part).wait_send()
    for step in range(1, frames):
        share(lax.rem(frame + step, frames), frame).wait_send()
    for which in range(2):
        for index in range(parts):

            @pl.when(frame < frames - 1)
            def _(which=which, index=index):
                side(which, 0, index).wait_send()

            @pl.when(frame > 0)
            def _(which=which, index=index):
                side(which, 1, index).wait_send()


def local(frames, parts, queries, key_tokens, values, near_list, near_count, dist_band, band_factor):
    _, rows, features = queries.shape
    far_rows = parts * rows // POOL
    far_total = frames * far_rows
    slots = near_list.shape[2]
    smem = pl.BlockSpec(memory_space=pltpu.SMEM)
    anywhere = pl.BlockSpec(memory_space=pl.ANY)
    dma = pltpu.SemaphoreType.DMA
    out = pl.pallas_call(
        functools.partial(kernel, frames, parts),
        out_shape=jax.ShapeDtypeStruct((rows, features), jnp.bfloat16),
        in_specs=[smem] * 4 + [anywhere] * 3,
        out_specs=pl.BlockSpec(memory_space=pltpu.VMEM),
        scratch_shapes=[
            pltpu.VMEM((3, parts, rows, HD), jnp.bfloat16),
            pltpu.VMEM((parts, rows, HD), jnp.bfloat16),
            pltpu.VMEM((3 * parts, rows, HD), jnp.bfloat16),
            pltpu.VMEM((3 * parts, rows, HD), jnp.bfloat16),
            pltpu.VMEM((parts, 8, HD), jnp.float32),
            pltpu.VMEM((frames, parts, 8, HD), jnp.float32),
            pltpu.VMEM((frames, far_rows, HD), jnp.float32),
            pltpu.VMEM((frames, far_rows, HD), jnp.float32),
            pltpu.VMEM((8, far_total), jnp.float32),
            pltpu.VMEM((rows, slots * rows), jnp.float32),
            pltpu.VMEM((parts, rows, slots * rows), jnp.bfloat16),
            pltpu.VMEM((parts, rows, far_total), jnp.bfloat16),
            pltpu.VMEM((parts, rows, HD), jnp.float32),
            pltpu.VMEM((parts, rows, HD), jnp.bfloat16),
            pltpu.VMEM((parts, rows, HD), jnp.bfloat16),
            dma((3,)),
            dma((3, parts)),
            dma((3, parts)),
            dma((3, parts)),
            dma((2, 2, parts)),
            dma((2, 2, parts)),
            dma((parts,)),
            dma((parts,)),
            dma((frames,)),
            dma((frames,)),
            dma((parts,)),
            dma((parts,)),
        ],
        compiler_params=pltpu.CompilerParams(
            collective_id=0, has_side_effects=True, vmem_limit_bytes=62 * 2**20
        ),
        cost_estimate=pl.CostEstimate(
            flops=4 * parts * rows * (slots * rows + far_total) * HD,
            bytes_accessed=8 * rows * features,
            transcendentals=parts * rows * (slots * rows + far_total),
        ),
    )(
        near_list,
        near_count.T,
        dist_band,
        band_factor,
        queries[0],
        key_tokens[0],
        values[0],
    )
    return out[None]


def solution(mesh):
    return jax.shard_map(
        functools.partial(local, mesh.shape["tm"], mesh.shape["space"]),
        mesh=mesh,
        in_specs=(
            P("tm", "space", None),
            P("tm", "space", None),
            P("tm", "space", None),
            P(),
            P(),
            P(),
            P(),
        ),
        out_specs=P("tm", "space", None),
        check_vma=False,
    )
```

```python
import functools
import math

import jax
import jax.numpy as jnp
from jax import lax
from jax.experimental import pallas as pl
from jax.experimental.pallas import tpu as pltpu
from jax.sharding import PartitionSpec as P

HD = 128
POOL = 128
LOWEST = -1e30
MESH = pl.DeviceIdType.MESH


def kernel(
    frames,
    parts,
    list_ref,
    count_ref,
    band_ref,
    factor_ref,
    q_ref,
    k_ref,
    v_ref,
    out_ref,
    heads,
    q_buf,
    k_buf,
    v_buf,
    pool_out,
    far_buf,
    far_k,
    far_v,
    far_bias,
    scores,
    near_weights,
    far_weights,
    totals,
    staged,
    returned,
    local_sem,
    head_sem,
    swap_send,
    swap_recv,
    side_send,
    side_recv,
    part_send,
    part_recv,
    pool_send,
    pool_recv,
    back_send,
    back_recv,
):
    frame = lax.axis_index("tm")
    part = lax.axis_index("space")
    rows = q_buf.shape[1]
    slots = list_ref.shape[2]
    each = rows // POOL
    far_rows = parts * each
    far_total = frames * far_rows
    steps = [(parts // 2 - 1 + i) % (parts - 1) + 1 for i in range(parts - 1)]

    def shifted(step):
        return lax.rem(part + step, parts)

    def columns(index):
        return pl.ds(pl.multiple_of(index * HD, HD), HD)

    sources = (k_ref, v_ref, q_ref)

    def landing(which, index):
        if which == 2:
            return q_buf.at[index]
        return (k_buf, v_buf)[which].at[parts + index]

    split = [
        [
            pltpu.make_async_copy(
                sources[which].at[:, head * HD : (head + 1) * HD],
                heads.at[which, head],
                head_sem.at[which, head],
            )
            for head in range(parts)
        ]
        for which in range(3)
    ]
    own = [
        pltpu.make_async_copy(
            sources[which].at[:, columns(part)], landing(which, part), local_sem.at[which]
        )
        for which in range(3)
    ]
    for which in (0, 2, 1):
        for copy in split[which] + [own[which]]:
            copy.start()

    barrier = pltpu.get_barrier_semaphore()
    for step in range(1, parts):
        pl.semaphore_signal(
            barrier, inc=1, device_id=(frame, shifted(step)), device_id_type=MESH
        )
    for step in range(1, frames):
        pl.semaphore_signal(
            barrier,
            inc=1,
            device_id=(lax.rem(frame + step, frames), part),
            device_id_type=MESH,
        )
    pl.semaphore_wait(barrier, parts - 1 + frames - 1)

    def swap(which, target, slot):
        return pltpu.make_async_remote_copy(
            src_ref=heads.at[which, target],
            dst_ref=landing(which, slot),
            send_sem=swap_send.at[which, target],
            recv_sem=swap_recv.at[which, slot],
            device_id=(frame, target),
            device_id_type=MESH,
        )

    def side(which, direction, index):
        there = index if direction == 0 else 2 * parts + index
        buf = (k_buf, v_buf)[which]
        target = frame + 1 if direction == 0 else frame - 1
        return pltpu.make_async_remote_copy(
            src_ref=buf.at[parts + index],
            dst_ref=buf.at[there],
            send_sem=side_send.at[direction, which, index],
            recv_sem=side_recv.at[direction, which, index],
            device_id=(target, part),
            device_id_type=MESH,
        )

    def forward(which, index):
        @pl.when(frame < frames - 1)
        def _():
            side(which, 0, index).start()

        @pl.when(frame > 0)
        def _():
            side(which, 1, index).start()

    def arrivals(which):
        for index in range(parts):

            @pl.when(frame > 0)
            def _(index=index):
                arrived = (k_buf, v_buf)[which].at[index]
                pltpu.make_async_remote_copy(
                    src_ref=arrived,
                    dst_ref=arrived,
                    send_sem=side_send.at[0, which, index],
                    recv_sem=side_recv.at[0, which, index],
                    device_id=(frame - 1, part),
                    device_id_type=MESH,
                ).wait_recv()

            @pl.when(frame < frames - 1)
            def _(index=index):
                arrived = (k_buf, v_buf)[which].at[2 * parts + index]
                pltpu.make_async_remote_copy(
                    src_ref=arrived,
                    dst_ref=arrived,
                    send_sem=side_send.at[1, which, index],
                    recv_sem=side_recv.at[1, which, index],
                    device_id=(frame + 1, part),
                    device_id_type=MESH,
                ).wait_recv()

    def spread(target, slot):
        return pltpu.make_async_remote_copy(
            src_ref=pool_out.at[target],
            dst_ref=far_buf.at[frame, slot],
            send_sem=part_send.at[target],
            recv_sem=part_recv.at[slot],
            device_id=(frame, target),
            device_id_type=MESH,
        )

    def share(target, slot):
        return pltpu.make_async_remote_copy(
            src_ref=far_buf.at[slot],
            dst_ref=far_buf.at[slot],
            send_sem=pool_send.at[target],
            recv_sem=pool_recv.at[slot],
            device_id=(target, part),
            device_id_type=MESH,
        )

    for copy in split[0]:
        copy.wait()
    for step in steps:
        swap(0, shifted(step), part).start()
    for which in (2, 1):
        for copy in split[which]:
            copy.wait()

    pool_row = lax.broadcasted_iota(jnp.int32, (8, rows), 0)
    pool_col = lax.broadcasted_iota(jnp.int32, (8, rows), 1) // POOL
    averages = [
        jnp.where(pool_row == pool_col + which * each, 1.0 / POOL, 0.0).astype(jnp.bfloat16)
        for which in range(2)
    ]
    for head in range(parts):
        pooled = sum(
            jnp.dot(averages[which], heads[which, head], preferred_element_type=jnp.float32)
            for which in range(2)
        )
        pool_out[head] = pooled.astype(jnp.bfloat16).astype(jnp.float32)
    far_buf[frame, part] = pool_out[part]
    for step in steps:
        spread(shifted(step), part).start()

    for which in (1, 2):
        for step in steps:
            swap(which, shifted(step), part).start()

    for which in range(2):
        own[which].wait()
        forward(which, part)
    for step in steps:
        source = shifted(parts - step)
        swap(0, source, source).wait_recv()
        forward(0, source)
    for step in steps:
        source = shifted(parts - step)
        spread(source, source).wait_recv()
    for step in range(1, frames):
        share(lax.rem(frame + step, frames), frame).start()
    for step in steps:
        source = shifted(parts - step)
        swap(1, source, source).wait_recv()
        forward(1, source)
    for step in range(1, frames):
        source = lax.rem(frame + step, frames)
        share(source, source).wait_recv()

    mix_row = lax.broadcasted_iota(jnp.int32, (far_rows, parts * 8), 0)
    mix_col = lax.broadcasted_iota(jnp.int32, (far_rows, parts * 8), 1)
    lane_frame = lax.broadcasted_iota(jnp.int32, (8, far_total), 1) // far_rows
    mixes = []
    for which in range(2):
        inner = mix_col % 8 - which * each
        held = (inner >= 0) & (inner < each)
        index = (mix_col // 8) * each + inner
        mixes.append(
            [
                jnp.where(held & (mix_row // e == index // e), 1.0 / e, 0.0)
                for e in (1, 2, 4)
            ]
        )
    bias = jnp.full((8, far_total), LOWEST, jnp.float32)
    for other in range(frames):
        distance = jnp.abs(frame - other)
        band = band_ref[distance]
        factor = jnp.int32(1)
        for entry in range(factor_ref.shape[0]):
            factor = jnp.where(band == entry + 1, factor_ref[entry], factor)
        offset = jnp.where(
            factor == 1,
            jnp.float32(0.0),
            jnp.where(factor == 2, jnp.float32(-math.log(2.0)), jnp.float32(-math.log(4.0))),
        )
        offset = jnp.where(distance >= 2, offset, jnp.float32(LOWEST))
        bias = jnp.where(lane_frame == other, offset, bias)
        pooled = far_buf[other].reshape(parts * 8, HD).astype(jnp.bfloat16)
        for which, far in enumerate((far_k, far_v)):
            once, pairs, quads = mixes[which]
            mix = jnp.where(factor == 1, once, jnp.where(factor == 2, pairs, quads))
            coarse = jnp.dot(
                mix.astype(jnp.bfloat16), pooled, preferred_element_type=jnp.float32
            )
            far[other] = coarse.astype(jnp.bfloat16).astype(jnp.float32)
    far_bias[...] = bias

    own[2].wait()
    for step in steps:
        source = shifted(parts - step)
        swap(2, source, source).wait_recv()
    arrivals(0)

    scale = 1.0 / math.sqrt(HD)
    contract = (((1,), (1,)), ((), ()))

    def weigh(block, carry):
        query = q_buf[block]
        live = count_ref[block, frame]
        far_scores = (
            lax.dot_general(
                query,
                far_k[...].reshape(far_total, HD).astype(jnp.bfloat16),
                contract,
                preferred_element_type=jnp.float32,
            )
            * scale
            + far_bias[0:1, :]
        )
        top = jnp.max(far_scores, axis=1, keepdims=True)
        for slot in range(slots):
            keys = k_buf[list_ref[frame, block, slot]]
            hidden = jnp.where(slot < live, jnp.float32(0.0), jnp.float32(LOWEST))
            near_scores = (
                lax.dot_general(query, keys, contract, preferred_element_type=jnp.float32) * scale
                + hidden
            )
            scores[:, slot * rows : (slot + 1) * rows] = near_scores
            top = jnp.maximum(top, jnp.max(near_scores, axis=1, keepdims=True))
        weights = jnp.exp(far_scores - top)
        total = jnp.sum(weights, axis=1, keepdims=True)
        far_weights[block] = weights.astype(jnp.bfloat16)
        for slot in range(slots):
            span = slice(slot * rows, (slot + 1) * rows)
            weights = jnp.exp(scores[:, span] - top)
            total = total + jnp.sum(weights, axis=1, keepdims=True)
            near_weights[block, :, span] = weights.astype(jnp.bfloat16)
        totals[block] = jnp.broadcast_to(total, (rows, HD))
        return carry


    arrivals(1)

    def attend(block):
        summed = jnp.dot(
            far_weights[block],
            far_v[...].reshape(far_total, HD).astype(jnp.bfloat16),
            preferred_element_type=jnp.float32,
        )
        for slot in range(slots):
            summed = summed + jnp.dot(
                near_weights[block, :, slot * rows : (slot + 1) * rows],
                v_buf[list_ref[frame, block, slot]],
                preferred_element_type=jnp.float32,
            )
        return (summed / totals[block]).astype(jnp.bfloat16)

    def back(target, slot):
        return pltpu.make_async_remote_copy(
            src_ref=staged.at[target],
            dst_ref=returned.at[slot],
            send_sem=back_send.at[target],
            recv_sem=back_recv.at[slot],
            device_id=(frame, target),
            device_id_type=MESH,
        )

    def one(i, carry):
        target = shifted((parts // 2 - 1 + i) % (parts - 1) + 1)
        weigh(target, 0)
        staged[target] = attend(target)
        back(target, part).start()
        return carry

    lax.fori_loop(0, parts - 1, one, 0)
    weigh(part, 0)
    returned[part] = attend(part)

    for step in steps:
        other = shifted(step)
        back(other, other).wait_recv()
    for head in range(parts):
        out_ref[:, head * HD : (head + 1) * HD] = returned[head]
    for step in steps:
        other = shifted(step)
        back(other, part).wait_send()
        spread(other, part).wait_send()
        for which in range(3):
            swap(which, other, part).wait_send()
    for step in range(1, frames):
        share(lax.rem(frame + step, frames), frame).wait_send()
    for which in range(2):
        for index in range(parts):

            @pl.when(frame < frames - 1)
            def _(which=which, index=index):
                side(which, 0, index).wait_send()

            @pl.when(frame > 0)
            def _(which=which, index=index):
                side(which, 1, index).wait_send()


def local(frames, parts, queries, key_tokens, values, near_list, near_count, dist_band, band_factor):
    _, rows, features = queries.shape
    far_rows = parts * rows // POOL
    far_total = frames * far_rows
    slots = near_list.shape[2]
    smem = pl.BlockSpec(memory_space=pltpu.SMEM)
    anywhere = pl.BlockSpec(memory_space=pl.ANY)
    dma = pltpu.SemaphoreType.DMA
    out = pl.pallas_call(
        functools.partial(kernel, frames, parts),
        out_shape=jax.ShapeDtypeStruct((rows, features), jnp.bfloat16),
        in_specs=[smem] * 4 + [anywhere] * 3,
        out_specs=pl.BlockSpec(memory_space=pltpu.VMEM),
        scratch_shapes=[
            pltpu.VMEM((3, parts, rows, HD), jnp.bfloat16),
            pltpu.VMEM((parts, rows, HD), jnp.bfloat16),
            pltpu.VMEM((3 * parts, rows, HD), jnp.bfloat16),
            pltpu.VMEM((3 * parts, rows, HD), jnp.bfloat16),
            pltpu.VMEM((parts, 8, HD), jnp.float32),
            pltpu.VMEM((frames, parts, 8, HD), jnp.float32),
            pltpu.VMEM((frames, far_rows, HD), jnp.float32),
            pltpu.VMEM((frames, far_rows, HD), jnp.float32),
            pltpu.VMEM((8, far_total), jnp.float32),
            pltpu.VMEM((rows, slots * rows), jnp.float32),
            pltpu.VMEM((parts, rows, slots * rows), jnp.bfloat16),
            pltpu.VMEM((parts, rows, far_total), jnp.bfloat16),
            pltpu.VMEM((parts, rows, HD), jnp.float32),
            pltpu.VMEM((parts, rows, HD), jnp.bfloat16),
            pltpu.VMEM((parts, rows, HD), jnp.bfloat16),
            dma((3,)),
            dma((3, parts)),
            dma((3, parts)),
            dma((3, parts)),
            dma((2, 2, parts)),
            dma((2, 2, parts)),
            dma((parts,)),
            dma((parts,)),
            dma((frames,)),
            dma((frames,)),
            dma((parts,)),
            dma((parts,)),
        ],
        compiler_params=pltpu.CompilerParams(
            collective_id=0, has_side_effects=True, vmem_limit_bytes=62 * 2**20
        ),
        cost_estimate=pl.CostEstimate(
            flops=4 * parts * rows * (slots * rows + far_total) * HD,
            bytes_accessed=8 * rows * features,
            transcendentals=parts * rows * (slots * rows + far_total),
        ),
    )(
        near_list,
        near_count.T,
        dist_band,
        band_factor,
        queries[0],
        key_tokens[0],
        values[0],
    )
    return out[None]


def solution(mesh):
    return jax.shard_map(
        functools.partial(local, mesh.shape["tm"], mesh.shape["space"]),
        mesh=mesh,
        in_specs=(
            P("tm", "space", None),
            P("tm", "space", None),
            P("tm", "space", None),
            P(),
            P(),
            P(),
            P(),
        ),
        out_specs=P("tm", "space", None),
        check_vma=False,
    )
```
